32 devices in a mesh: seq: 8 (over y, x, core), wa: 4 (over z).
Axes of the slice: x: 2, y: 2, z: 4, core: 2. Of those that a mesh axis runs over, the one named last changes fastest.
Arguments:
- hidden_in: bfloat16 [4096, 2048], P('seq', 'wa'), may hold values from -6 to 6
- request_spans: int32 [4, 2], replicated, may hold values from 0 to 4096, as said below
- owners: int32 [4], replicated, may hold values from 0 to 7, as said below
- mixer_gain: float32 [2048], replicated, may hold values from 0.1 to 1.9
- query_weight: bfloat16 [2048, 2048], P(None, 'wa'), may hold values from -0.125 to 0.125
- forget_weight: bfloat16 [2048, 2048], P(None, 'wa'), may hold values from -0.0625 to 0.0625
- input_weight: bfloat16 [2048, 2048], P(None, 'wa'), may hold values from -0.125 to 0.125
- gate_weight: bfloat16 [2048, 2048], P(None, 'wa'), may hold values from -0.125 to 0.125
- forget_bias: float32 [2048], P('wa')
- output_weight: bfloat16 [2048, 2048], P('wa'), may hold values from -0.125 to 0.125
- swiglu_gain: float32 [2048], replicated, may hold values from 0.1 to 1.9
- swiglu_gate: bfloat16 [2048, 3072], P(None, 'wa'), may hold values from -0.125 to 0.125
- swiglu_up: bfloat16 [2048, 3072], P(None, 'wa'), may hold values from -0.125 to 0.125
- swiglu_down: bfloat16 [3072, 2048], P('wa'), may hold values from -0.109375 to 0.109375
Outputs:
- hidden_out: bfloat16 [4096, 2048], P('seq', 'wa')
- handed_state: float32 [8, 16, 128, 128], P('seq', 'wa')
The draws below stay inside these ranges and needn't reach their ends.
Inputs may be any that keep to these rules, and one draw needn't show every extreme that they name: Requests lie back to back in order: request_spans[0, 0] = 0, each request's end equals the next one's start, the last end is 4096, and every request holds at least 64 tokens. The owners are distinct indices along seq; the last request's owner is the index half of 8 minus one; the first request's owner is the index just before that of the device holding the first request's last token, counted round; the index 7 is always an owner.
All inputs are finite; a program needn't handle non-finite values.
Results may differ from the reference program's by a relative error of at most 0.009.
Values may be sent and summed in bfloat16 or wider, within the bound.
A program may use at most 128 MiB of HBM per device.

```python
import jax
import jax.numpy as jnp
from jax import lax

D = 2048
H = 16
HEAD = 128
FF = 3072
GROUP = 64
REQS = 4
TOK_DEV = 512
TOKENS = 4096
N_SEQ = 8


def draw_request_spans(key, part):
    key_length, key_place = jax.random.split(key)
    lowest = max(GROUP, TOK_DEV // 4)
    shorter = jax.random.randint(key_length, (REQS,), lowest, lowest + TOK_DEV // 2 + 1)
    long_place = jax.random.randint(key_place, (), 0, REQS)
    ranks = jnp.arange(REQS)
    others = jnp.sum(jnp.where(ranks == long_place, 0, shorter))
    lengths = jnp.where(ranks == long_place, TOKENS - others, shorter).astype(jnp.int32)
    end_rows = jnp.cumsum(lengths).astype(jnp.int32)
    return jnp.stack([end_rows - lengths, end_rows], axis=1).astype(jnp.int32)


def draw_owners(key, part):
    spans = draw_request_spans(key, part)
    across = N_SEQ // 2 - 1
    first_device = ((spans[0, 1] - 1) // TOK_DEV).astype(jnp.int32)
    first_owner = jnp.where(first_device == 0, N_SEQ - 1, first_device - 1).astype(jnp.int32)
    shuffled = jax.random.permutation(jax.random.fold_in(key, 7), N_SEQ).astype(jnp.int32)
    ranked = jnp.arange(N_SEQ, dtype=jnp.int32)
    taken = (ranked == first_owner) | (ranked == across)
    scores = jnp.where(taken, N_SEQ + ranked, jnp.where(ranked == N_SEQ - 1, -1, shuffled)).astype(jnp.int32)
    picked = jnp.argsort(scores, stable=True)[:REQS - 2].astype(jnp.int32)
    return jnp.concatenate([first_owner[None], picked, jnp.array([across], jnp.int32)]).astype(jnp.int32)


def draw_forget_bias(key, part):
    key_head, key_rate = jax.random.split(key)
    picked = jax.random.uniform(key_head, (H,), jnp.float32)
    slow_heads = picked < 0.5
    slow_mask = jnp.repeat(slow_heads, HEAD)
    placing = jax.random.uniform(key_rate, (H * HEAD,), jnp.float32)
    slow_rate = jnp.exp(jnp.log(0.3 / TOKENS) + placing * jnp.log(2.0 / 0.3))
    fast_rate = jnp.exp(jnp.log(1.0 / 30.0) - placing * jnp.log(TOK_DEV / 30.0))
    chosen_rate = jnp.where(slow_mask, slow_rate, fast_rate)
    return jnp.log(1.0 / chosen_rate - 1.0).astype(jnp.float32)


def block_levels(rng, shape, cuts, least, largest):
    def one(dim, blocks):
        steps = jax.random.uniform(jax.random.fold_in(jax.random.fold_in(rng, 6), dim), (blocks,), jnp.float32, least / len(cuts), largest / len(cuts))
        return jnp.repeat(jnp.exp(steps), shape[dim] // blocks).reshape((-1,) + (1,) * (len(shape) - dim - 1))

    level = one(*cuts[0])
    for cut in cuts[1:]:
        level = level * one(*cut)
    return level


def gaussian(rng, dims, deviation, limit, cuts=(), held_as=jnp.bfloat16):
    gain = block_levels(rng, dims, cuts, -0.22, 0.18) if cuts else 1.0
    values = jax.random.normal(rng, dims, jnp.float32) * deviation * gain
    return jnp.minimum(jnp.maximum(values, -limit), limit).astype(held_as)


def setup_inputs(seed: int = 0) -> dict:
    arg_keys = jax.random.split(jax.random.key(seed), 15)
    hidden_in = gaussian(arg_keys[0], (TOKENS, D), 1.0, 6.0, ((0, 8), (1, 4)))
    request_spans = draw_request_spans(jax.random.fold_in(arg_keys[14], 71), 0)
    owners = draw_owners(jax.random.fold_in(arg_keys[14], 71), 0)
    mixer_gain = jnp.clip(1.0 + 0.18 * jax.random.normal(arg_keys[3], (D,), jnp.float32), 0.1, 1.9)
    query_weight = gaussian(arg_keys[4], (D, D), D ** -0.5, 0.125, ((1, 4),))
    forget_weight = gaussian(arg_keys[5], (D, D), (4 * D) ** -0.5, 0.0625, ((1, 4),))
    input_weight = gaussian(arg_keys[6], (D, D), D ** -0.5, 0.125, ((1, 4),))
    gate_weight = gaussian(arg_keys[7], (D, D), D ** -0.5, 0.125, ((1, 4),))
    forget_bias = draw_forget_bias(jax.random.fold_in(arg_keys[14], 71), 0)
    output_weight = gaussian(arg_keys[9], (D, D), D ** -0.5, 0.125, ((0, 4),))
    swiglu_gain = jnp.clip(1.0 + 0.18 * jax.random.normal(arg_keys[10], (D,), jnp.float32), 0.1, 1.9)
    swiglu_gate = gaussian(arg_keys[11], (D, FF), D ** -0.5, 0.125, ((1, 4),))
    swiglu_up = gaussian(arg_keys[12], (D, FF), D ** -0.5, 0.125, ((1, 4),))
    swiglu_down = gaussian(arg_keys[13], (FF, D), FF ** -0.5, 0.109375, ((0, 4),))
    return dict(hidden_in=hidden_in, request_spans=request_spans, owners=owners, mixer_gain=mixer_gain, query_weight=query_weight, forget_weight=forget_weight, input_weight=input_weight, gate_weight=gate_weight, forget_bias=forget_bias, output_weight=output_weight, swiglu_gain=swiglu_gain, swiglu_gate=swiglu_gate, swiglu_up=swiglu_up, swiglu_down=swiglu_down)


EPS = 1e-06
HIGH = lax.Precision.HIGHEST

def rms_rows(matrix, scaling):
    matrix = matrix.astype(jnp.float32)
    rescale = lax.rsqrt(lax.optimization_barrier(jnp.mean(matrix * matrix, axis=-1, keepdims=True)) + EPS)
    return (matrix * rescale * scaling).astype(jnp.bfloat16)

def project(matrix, weight):
    return jnp.dot(matrix, weight, preferred_element_type=jnp.float32)

def reference(hidden_in, request_spans, owners, mixer_gain, query_weight, forget_weight, input_weight, gate_weight, forget_bias, output_weight, swiglu_gain, swiglu_gate, swiglu_up, swiglu_down):
    normed = rms_rows(hidden_in, mixer_gain)
    queries = jax.nn.silu(project(normed, query_weight))
    forget_logit = project(normed, forget_weight) + forget_bias
    log_decay = jax.nn.log_sigmoid(forget_logit)
    key_rows = jax.nn.sigmoid(-forget_logit)
    value_rows = project(normed, input_weight)
    gate_logit = project(normed, gate_weight)
    position = jnp.arange(TOKENS, dtype=jnp.int32)
    start_rows = request_spans[:, 0].astype(jnp.int32)
    end_rows = request_spans[:, 1].astype(jnp.int32)
    is_start = jnp.any(position[:, None] == start_rows[None, :], axis=1)
    segment = (lax.optimization_barrier(jnp.sum((start_rows[None, :] <= position[:, None]).astype(jnp.int32), axis=1)) - 1).astype(jnp.int32)
    block_count = TOKENS // GROUP
    shape_four = (block_count, GROUP, H, HEAD)
    scanned = (queries.reshape(shape_four), log_decay.reshape(shape_four), key_rows.reshape(shape_four), value_rows.reshape(shape_four), segment.reshape(block_count, GROUP), (1.0 - is_start.astype(jnp.float32)).reshape(block_count, GROUP), jnp.arange(block_count, dtype=jnp.int32) * GROUP)
    offsets = jnp.arange(GROUP, dtype=jnp.int32)
    causal = offsets[:, None] >= offsets[None, :]

    def advance(carried, blocked):
        running, handed = carried
        query_part, decay_part, key_part, value_part, segment_part, keep_mask, first_row = blocked
        cum_decay = jnp.cumsum(decay_part, axis=0)
        surviving = jnp.cumprod(keep_mask)
        query_tilde = query_part * jnp.exp(cum_decay)
        key_tilde = key_part * jnp.exp(-cum_decay)
        same_doc = causal & (segment_part[:, None] == segment_part[None, :])
        scores = jnp.einsum('ihc,jhc->hij', query_tilde, key_tilde, precision=HIGH)
        scores = jnp.where(same_doc[None], scores, 0.0)
        result = jnp.einsum('hij,jhd->ihd', scores, value_part, precision=HIGH)
        result = result + surviving[:, None, None] * jnp.einsum('ihc,hcd->ihd', query_tilde, running, precision=HIGH)
        tail_mask = (segment_part == segment_part[-1]).astype(jnp.float32)
        fresh = jnp.einsum('jhc,jhd->hcd', key_tilde * tail_mask[:, None, None], value_part, precision=HIGH)
        new_state = jnp.exp(cum_decay[-1])[:, :, None] * (surviving[-1] * running + fresh)
        local_end = (end_rows - 1 - first_row).astype(jnp.int32)
        inside = (local_end >= 0) & (local_end < GROUP)
        end_row = jnp.sum(jnp.where(inside, local_end, 0)).astype(jnp.int32)
        decay_end = lax.dynamic_index_in_dim(cum_decay, end_row, 0, keepdims=False)
        segment_end = lax.dynamic_index_in_dim(segment_part, end_row, 0, keepdims=False)
        alive_end = lax.dynamic_index_in_dim(surviving, end_row, 0, keepdims=False)
        upto_mask = ((offsets <= end_row) & (segment_part == segment_end)).astype(jnp.float32)
        partial_end = jnp.einsum('jhc,jhd->hcd', key_tilde * upto_mask[:, None, None], value_part, precision=HIGH)
        end_state = jnp.exp(decay_end)[:, :, None] * (alive_end * running + partial_end)
        handed = handed + inside.astype(jnp.float32)[:, None, None, None] * end_state[None]
        return ((new_state, handed), result)
    zero_state = jnp.zeros((H, HEAD, HEAD), jnp.float32)
    zero_handed = jnp.zeros((REQS, H, HEAD, HEAD), jnp.float32)
    (final_state, handed), outputs = lax.scan(advance, (zero_state, zero_handed), scanned)
    mixer_out = outputs.reshape(TOKENS, H, HEAD)
    rescale = lax.rsqrt(lax.optimization_barrier(jnp.mean(mixer_out * mixer_out, axis=-1, keepdims=True)) + EPS)
    mixed_rows = (mixer_out * rescale * jax.nn.silu(gate_logit.reshape(TOKENS, H, HEAD))).reshape(TOKENS, D).astype(jnp.bfloat16)
    residual = (hidden_in.astype(jnp.float32) + project(mixed_rows, output_weight)).astype(jnp.bfloat16)
    normed_ffn = rms_rows(residual, swiglu_gain)
    hidden = (jax.nn.silu(project(normed_ffn, swiglu_gate)) * project(normed_ffn, swiglu_up)).astype(jnp.bfloat16)
    hidden_out = (residual.astype(jnp.float32) + project(hidden, swiglu_down)).astype(jnp.bfloat16)
    handed_state = jnp.zeros((N_SEQ, H, HEAD, HEAD), jnp.float32).at[owners.astype(jnp.int32)].set(handed)
    return (hidden_out, handed_state)
```

```python
import jax
import jax.numpy as jnp
from jax import lax
from jax.experimental import pallas as pl
from jax.experimental.pallas import tpu as pltpu
from jax.sharding import PartitionSpec as P

HEAD = 128
GROUP = 64
REQS = 4
CHUNKS = 4
EPS = 1e-06
HIGH = lax.Precision.HIGHEST
MESH = pl.DeviceIdType.MESH
BF = jnp.bfloat16
F32 = jnp.float32
VMEM_BYTES = 58 * 1024 * 1024


def dot(a, b, contract=(1, 0), precision=None):
    return lax.dot_general(
        a, b, (((contract[0],), (contract[1],)), ((), ())), precision=precision,
        preferred_element_type=F32,
    )


def inside(index, count):
    return (index >= 0) & (index < count)


def greet_wa(me, count, barrier):
    for sgn in (1, -1):
        @pl.when(inside(me + sgn, count))
        def _():
            pl.semaphore_signal(barrier, inc=1, device_id={"wa": me + sgn}, device_id_type=MESH)


class Gather:
    def __init__(self, buf, send_sem, recv_sem, me, count, rows):
        self.buf, self.send_sem, self.recv_sem = buf, send_sem, recv_sem
        self.me, self.count, self.rows = me, count, rows

    def copy(self, src, c, sgn, target):
        ref = self.buf.at[src, pl.ds(c * self.rows, self.rows)]
        return pltpu.make_async_remote_copy(
            src_ref=ref, dst_ref=ref,
            send_sem=self.send_sem.at[(sgn + 1) // 2, src, c],
            recv_sem=self.recv_sem.at[src, c],
            device_id={"wa": target}, device_id_type=MESH,
        )

    def own(self, c):
        for sgn in (1, -1):
            @pl.when(inside(self.me + sgn, self.count))
            def _():
                self.copy(self.me, c, sgn, self.me + sgn).start()

    def arrive(self, c):
        for k in range(1, self.count):
            for sgn in (1, -1):
                src = self.me - sgn * k

                @pl.when(inside(src, self.count))
                def _():
                    self.copy(src, c, sgn, self.me - sgn).wait_recv()

                    @pl.when(inside(self.me + sgn, self.count))
                    def _():
                        self.copy(src, c, sgn, self.me + sgn).start()

    def drain(self):
        for c in range(CHUNKS):
            for k in range(self.count):
                for sgn in (1, -1):
                    src = self.me - sgn * k

                    @pl.when(inside(src, self.count) & inside(self.me + sgn, self.count))
                    def _():
                        self.copy(src, c, sgn, self.me + sgn).wait_send()


class Scatter:
    def __init__(self, part, out, came, send_sem, recv_sem, me, count, rows):
        self.part, self.out, self.came = part, out, came
        self.send_sem, self.recv_sem = send_sem, recv_sem
        self.me, self.count, self.rows = me, count, rows
        first = jnp.where(2 * me < count, 1, -1)
        self.ways = (first, -first)

    def copy(self, w, c, sgn, target):
        span = pl.ds(c * self.rows, self.rows)
        way = (sgn + 1) // 2
        return pltpu.make_async_remote_copy(
            src_ref=self.out.at[w, span], dst_ref=self.came.at[way, w, span],
            send_sem=self.send_sem.at[w, c], recv_sem=self.recv_sem.at[way, w, c],
            device_id={"wa": target}, device_id_type=MESH,
        )

    def hop(self, c):
        span = pl.ds(c * self.rows, self.rows)
        me, count = self.me, self.count
        for sgn in self.ways:
            way = (sgn + 1) // 2
            for k in range(count - 1, 0, -1):
                w = me + sgn * k

                @pl.when(inside(w, count))
                def _():
                    @pl.when(inside(me - sgn, count))
                    def _():
                        self.copy(w, c, sgn, me - sgn).wait_recv()
                        self.out[w, span] = (
                            self.part[w, span] + self.came[way, w, span].astype(F32)
                        ).astype(BF)

                    @pl.when(jnp.logical_not(inside(me - sgn, count)))
                    def _():
                        self.out[w, span] = self.part[w, span].astype(BF)

                    self.copy(w, c, sgn, me + sgn).start()

    def total(self, c):
        span = pl.ds(c * self.rows, self.rows)
        me, count = self.me, self.count
        for sgn in self.ways:
            way = (sgn + 1) // 2

            @pl.when(inside(me - sgn, count))
            def _():
                self.copy(me, c, sgn, me - sgn).wait_recv()
                self.part[me, span] = self.part[me, span] + self.came[way, me, span].astype(F32)
        return self.part[me, span]

    def drain(self):
        for c in range(CHUNKS):
            for sgn in (1, -1):
                for k in range(1, self.count):
                    w = self.me + sgn * k

                    @pl.when(inside(w, self.count))
                    def _():
                        self.copy(w, c, sgn, self.me + sgn).wait_send()


def rms_chunk(buf, count, c, rows, gain):
    span = pl.ds(c * rows, rows)
    pieces = [buf[s, span].astype(F32) for s in range(count)]
    width = pieces[0].shape[1]
    square = sum(jnp.sum(piece * piece, axis=1, keepdims=True) for piece in pieces)
    rescale = lax.rsqrt(square / (width * count) + EPS)
    return jnp.concatenate(
        [
            (piece * rescale * gain[:, s * width:(s + 1) * width]).astype(BF)
            for s, piece in enumerate(pieces)
        ],
        axis=1,
    )


def silu(v):
    return v / (1.0 + jnp.exp(-v))


def enter_kernel(
    hidden, gain, bias, wq, wf, wi, wg,
    q_out, ld_out, k_out, v_out, g_out,
    buf, vq, vf, vi, vg, w_sem, own_sem, send_sem, recv_sem,
):
    me, count = lax.axis_index("wa"), lax.axis_size("wa")
    rows = hidden.shape[0] // CHUNKS
    loads = [
        pltpu.make_async_copy(src, dst, w_sem.at[i])
        for i, (src, dst) in enumerate(((wq, vq), (wf, vf), (wi, vi), (wg, vg)))
    ]
    mine = pltpu.make_async_copy(hidden, buf.at[me], own_sem)
    mine.start()
    barrier = pltpu.get_barrier_semaphore()
    greet_wa(me, count, barrier)
    mine.wait()
    near = inside(me - 1, count).astype(jnp.int32) + inside(me + 1, count).astype(jnp.int32)
    pl.semaphore_wait(barrier, near)
    ag = Gather(buf, send_sem, recv_sem, me, count, rows)
    ag.own(0)
    ag.own(1)
    for load in loads:
        load.start()
    for c in range(CHUNKS):
        ag.arrive(c)
        if c + 2 < CHUNKS:
            ag.own(c + 2)
        if c == 0:
            for load in loads:
                load.wait()
        span = pl.ds(c * rows, rows)
        normed = rms_chunk(buf, count, c, rows, gain[...])
        q_out[span] = silu(dot(normed, vq[...]))
        logit = dot(normed, vf[...]) + bias[...]
        ld_out[span] = jnp.minimum(logit, 0.0) - jnp.log1p(jnp.exp(-jnp.abs(logit)))
        k_out[span] = 1.0 / (1.0 + jnp.exp(logit))
        v_out[span] = dot(normed, vi[...]).astype(BF)
        g_out[span] = silu(dot(normed, vg[...]))
    ag.drain()


def block_kernel(
    spans, first_ref, q, ld, k, v,
    out, qp, state_out, decay_out, ends, end_decay,
    state, decay,
):
    heads = q.shape[1] // HEAD
    blocks = q.shape[0] // GROUP
    state[...] = jnp.zeros_like(state)
    decay[...] = jnp.ones_like(decay)
    ends[...] = jnp.zeros_like(ends)
    end_decay[...] = jnp.zeros_like(end_decay)
    below = lax.broadcasted_iota(jnp.int32, (GROUP, GROUP), 0)
    across = lax.broadcasted_iota(jnp.int32, (GROUP, GROUP), 1)
    causal = below >= across
    lower = causal.astype(F32)
    column = lax.broadcasted_iota(jnp.int32, (GROUP, 1), 0)
    line = lax.broadcasted_iota(jnp.int32, (1, GROUP), 1)

    def began(position):
        return sum((spans[r, 0] <= position).astype(jnp.int32) for r in range(REQS))

    def body(n, carry):
        rows = pl.ds(pl.multiple_of(n * GROUP, GROUP), GROUP)
        base = first_ref[0] + n * GROUP
        cum = dot(lower, ld[rows], precision=HIGH)
        qt = q[rows] * jnp.exp(cum)
        kt = k[rows] * jnp.exp(-cum)
        vb = v[rows]
        seg = began(base + column)
        mask = causal & (seg == began(base + line))
        prev, last = began(base - 1), began(base + GROUP - 1)
        surviving = (seg == prev).astype(F32)
        tail = (seg == last).astype(F32)
        alive = (last == prev).astype(F32)
        for r in range(REQS):
            within = spans[r, 1] - 1 - base

            @pl.when((within >= 0) & (within < GROUP))
            def _():
                upto = ((column <= within) & (seg == r + 1)).astype(F32)
                alive_end = (prev == r + 1).astype(F32)
                at_end = jnp.exp(
                    jnp.sum(jnp.where(column == within, cum, 0.0), axis=0, keepdims=True)
                )
                for h in range(heads):
                    hs = slice(h * HEAD, (h + 1) * HEAD)
                    partial = dot(vb[:, hs], (kt[:, hs] * upto).astype(BF), (0, 0))
                    ends[r, h] = at_end[:, hs] * (alive_end * state[h] + partial)
                    end_decay[r, h:h + 1] = at_end[:, hs] * alive_end * decay[h:h + 1]

        for h in range(heads):
            hs = slice(h * HEAD, (h + 1) * HEAD)
            qh, vh = qt[:, hs].astype(BF), vb[:, hs]
            scores = dot(qh, kt[:, hs].astype(BF), (1, 1))
            scores = jnp.where(mask, scores, 0.0).astype(BF)
            held, shrunk = state[h], decay[h:h + 1]
            out[rows, hs] = dot(scores, vh) + surviving * dot(qh, held.astype(BF), (1, 1))
            qp[rows, hs] = (qt[:, hs] * surviving * shrunk).astype(BF)
            fresh = dot(vh, (kt[:, hs] * tail).astype(BF), (0, 0))
            full = jnp.exp(cum[GROUP - 1:GROUP, hs])
            state[h] = full * (alive * held + fresh)
            decay[h:h + 1] = shrunk * (full * alive)
        return carry

    lax.fori_loop(0, blocks, body, 0)
    state_out[...] = state[...].astype(BF)
    decay_out[...] = decay[...]


def leave_kernel(
    owners, hidden, out_local, qp, g, state, decay, ends, end_decay, gain, wo, wgate, wup, wdown,
    y_out, handed_out,
    vo, vgate, vup, vdown, part1, part2, out1, out2, came1, came2, buf,
    states, decays, incoming, end_mine, end_out, end_came,
    w_sem, rs1_send, rs1_recv, rs2_send, rs2_recv, ag_send, ag_recv,
    st_send, st_recv, de_send, de_recv, en_send, en_recv,
):
    me, count = lax.axis_index("wa"), lax.axis_size("wa")
    place, places = lax.axis_index("seq"), lax.axis_size("seq")
    rows = hidden.shape[0] // CHUNKS
    width = hidden.shape[1]
    heads = width // HEAD
    loads = [
        pltpu.make_async_copy(src, dst, w_sem.at[i])
        for i, (src, dst) in enumerate(((wo, vo), (wgate, vgate), (wup, vup), (wdown, vdown)))
    ]
    barrier = pltpu.get_barrier_semaphore()
    greet_wa(me, count, barrier)

    def others(act):
        def step(j, carry):
            act(lax.rem(place + j, places))
            return carry
        lax.fori_loop(1, places, step, 0)

    others(lambda peer: pl.semaphore_signal(
        barrier, inc=1, device_id={"seq": peer}, device_id_type=MESH))
    near = inside(me - 1, count).astype(jnp.int32) + inside(me + 1, count).astype(jnp.int32)
    pl.semaphore_wait(barrier, near + (places - 1))

    def state_copy(source, peer, send):
        return pltpu.make_async_remote_copy(
            src_ref=state, dst_ref=states.at[source], send_sem=st_send.at[send],
            recv_sem=st_recv.at[source], device_id={"seq": peer}, device_id_type=MESH)

    def decay_copy(source, peer, send):
        return pltpu.make_async_remote_copy(
            src_ref=decay, dst_ref=decays.at[source], send_sem=de_send.at[send],
            recv_sem=de_recv.at[source], device_id={"seq": peer}, device_id_type=MESH)

    def end_copy(source, peer, send):
        return pltpu.make_async_remote_copy(
            src_ref=end_out.at[send], dst_ref=end_came.at[source], send_sem=en_send.at[send],
            recv_sem=en_recv.at[source], device_id={"seq": peer}, device_id_type=MESH)

    def later(act):
        def step(peer, carry):
            act(peer)
            return carry
        lax.fori_loop(place + 1, places, step, 0)

    def push(peer):
        state_copy(place, peer, peer).start()
        decay_copy(place, peer, peer).start()

    later(push)
    for load in loads:
        load.start()
    incoming[...] = jnp.zeros_like(incoming)

    def join(p, carry):
        state_copy(p, p, p).wait_recv()
        decay_copy(p, p, p).wait_recv()
        for h in range(heads):
            incoming[h] = incoming[h] * decays[p, h:h + 1] + states[p, h].astype(F32)
        return carry

    lax.fori_loop(0, place, join, 0)
    loads[0].wait()

    rs1 = Scatter(part1, out1, came1, rs1_send, rs1_recv, me, count, rows)
    rs2 = Scatter(part2, out2, came2, rs2_send, rs2_recv, me, count, rows)
    ag = Gather(buf, ag_send, ag_recv, me, count, rows)

    def mix(c):
        span = pl.ds(c * rows, rows)
        mixed = []
        for h in range(heads):
            hs = slice(h * HEAD, (h + 1) * HEAD)
            o = out_local[span, hs] + dot(qp[span, hs], incoming[h].astype(BF), (1, 1))
            rescale = lax.rsqrt(jnp.mean(o * o, axis=1, keepdims=True) + EPS)
            mixed.append((o * rescale * g[span, hs]).astype(BF))
        mixed = jnp.concatenate(mixed, axis=1)
        for w in range(count):
            part1[w, span] = dot(mixed, vo[:, w * width:(w + 1) * width])

    def settle(c):
        span = pl.ds(c * rows, rows)
        rs1.hop(c)
        buf[me, span] = (hidden[span].astype(F32) + rs1.total(c)).astype(BF)
        ag.own(c)

    def feed(c):
        span = pl.ds(c * rows, rows)
        ag.arrive(c)
        normed = rms_chunk(buf, count, c, rows, gain[...])
        units = (silu(dot(normed, vgate[...])) * dot(normed, vup[...])).astype(BF)
        for w in range(count):
            part2[w, span] = dot(units, vdown[:, w * width:(w + 1) * width])

    def finish(c):
        span = pl.ds(c * rows, rows)
        rs2.hop(c)
        y_out[span] = (buf[me, span].astype(F32) + rs2.total(c)).astype(BF)

    def hand_over():
        for r in range(REQS):
            for h in range(heads):
                end_mine[r, h] = ends[r, h] + end_decay[r, h:h + 1] * incoming[h]

        def fill(peer, carry):
            picks = [(owners[r] == peer).astype(F32) for r in range(REQS)]
            for h in range(heads):
                end_out[peer, h] = sum(picks[r] * end_mine[r, h] for r in range(REQS)).astype(BF)
            return carry

        lax.fori_loop(0, places, fill, 0)
        others(lambda peer: end_copy(place, peer, peer).start())

    mix(0)
    mix(1)
    settle(0)
    mix(2)
    settle(1)
    mix(3)
    hand_over()
    settle(2)
    for load in loads[1:]:
        load.wait()
    feed(0)
    settle(3)
    feed(1)
    finish(0)
    feed(2)
    finish(1)
    feed(3)
    finish(2)
    finish(3)

    others(lambda peer: end_copy(peer, peer, peer).wait_recv())
    end_came[place] = end_out[place]
    for h in range(heads):
        def gather_end(p, total):
            return total + end_came[p, h].astype(F32)
        handed_out[0, h] = lax.fori_loop(
            0, places, gather_end, jnp.zeros((HEAD, HEAD), F32)).T
    others(lambda peer: end_copy(place, peer, peer).wait_send())

    def sent(peer):
        state_copy(place, peer, peer).wait_send()
        decay_copy(place, peer, peer).wait_send()

    later(sent)
    rs1.drain()
    rs2.drain()
    ag.drain()


def local(
    hidden_in, request_spans, owners, mixer_gain, query_weight, forget_weight, input_weight,
    gate_weight, forget_bias, output_weight, swiglu_gain, swiglu_gate, swiglu_up, swiglu_down,
):
    count, places = lax.axis_size("wa"), lax.axis_size("seq")
    tok, width = hidden_in.shape
    heads = width // HEAD
    depth = query_weight.shape[0]
    ff = swiglu_gate.shape[1]
    vmem = pl.BlockSpec(memory_space=pltpu.VMEM)
    smem = pl.BlockSpec(memory_space=pltpu.SMEM)
    hbm = pl.BlockSpec(memory_space=pl.ANY)
    DMA = pltpu.SemaphoreType.DMA

    q, ld, k, v, g = pl.pallas_call(
        enter_kernel,
        out_shape=[jax.ShapeDtypeStruct((tok, width), t) for t in (F32, F32, F32, BF, F32)],
        in_specs=[vmem] * 3 + [hbm] * 4,
        out_specs=[vmem] * 5,
        scratch_shapes=[pltpu.VMEM((count, tok, width), BF)]
        + [pltpu.VMEM((depth, width), BF)] * 4
        + [DMA((4,)), DMA, DMA((2, count, CHUNKS)), DMA((count, CHUNKS))],
        compiler_params=pltpu.CompilerParams(
            collective_id=0, has_side_effects=True, vmem_limit_bytes=VMEM_BYTES),
        name="enter",
    )(
        hidden_in, mixer_gain[None], forget_bias[None],
        query_weight, forget_weight, input_weight, gate_weight,
    )

    first = (lax.axis_index("seq") * tok).astype(jnp.int32)[None]
    out_local, qp, state, decay, ends, end_decay = pl.pallas_call(
        block_kernel,
        out_shape=[
            jax.ShapeDtypeStruct((tok, width), F32),
            jax.ShapeDtypeStruct((tok, width), BF),
            jax.ShapeDtypeStruct((heads, HEAD, HEAD), BF),
            jax.ShapeDtypeStruct((heads, HEAD), F32),
            jax.ShapeDtypeStruct((REQS, heads, HEAD, HEAD), F32),
            jax.ShapeDtypeStruct((REQS, heads, HEAD), F32),
        ],
        in_specs=[smem, smem] + [vmem] * 4,
        out_specs=[vmem] * 6,
        scratch_shapes=[pltpu.VMEM((heads, HEAD, HEAD), F32), pltpu.VMEM((heads, HEAD), F32)],
        compiler_params=pltpu.CompilerParams(vmem_limit_bytes=VMEM_BYTES),
        name="blocks",
    )(request_spans, first, q, ld, k, v)

    y, handed = pl.pallas_call(
        leave_kernel,
        out_shape=[
            jax.ShapeDtypeStruct((tok, width), BF),
            jax.ShapeDtypeStruct((1, heads, HEAD, HEAD), F32),
        ],
        in_specs=[smem] + [vmem] * 9 + [hbm] * 4,
        out_specs=[vmem] * 2,
        scratch_shapes=[
            pltpu.VMEM((width, depth), BF),
            pltpu.VMEM((depth, ff), BF),
            pltpu.VMEM((depth, ff), BF),
            pltpu.VMEM((ff, depth), BF),
            pltpu.VMEM((count, tok, width), F32),
            pltpu.VMEM((count, tok, width), F32),
            pltpu.VMEM((count, tok, width), BF),
            pltpu.VMEM((count, tok, width), BF),
            pltpu.VMEM((2, count, tok, width), BF),
            pltpu.VMEM((2, count, tok, width), BF),
            pltpu.VMEM((count, tok, width), BF),
            pltpu.VMEM((places, heads, HEAD, HEAD), BF),
            pltpu.VMEM((places, heads, HEAD), F32),
            pltpu.VMEM((heads, HEAD, HEAD), F32),
            pltpu.VMEM((REQS, heads, HEAD, HEAD), F32),
            pltpu.VMEM((places, heads, HEAD, HEAD), BF),
            pltpu.VMEM((places, heads, HEAD, HEAD), BF),
            DMA((4,)),
            DMA((count, CHUNKS)), DMA((2, count, CHUNKS)),
            DMA((count, CHUNKS)), DMA((2, count, CHUNKS)),
            DMA((2, count, CHUNKS)), DMA((count, CHUNKS)),
            DMA((places,)), DMA((places,)), DMA((places,)), DMA((places,)),
            DMA((places,)), DMA((places,)),
        ],
        compiler_params=pltpu.CompilerParams(
            collective_id=1, has_side_effects=True, vmem_limit_bytes=VMEM_BYTES),
        name="leave",
    )(
        owners, hidden_in, out_local, qp, g, state, decay, ends, end_decay,
        swiglu_gain[None], output_weight, swiglu_gate, swiglu_up, swiglu_down,
    )
    return y, handed


def solution(mesh):
    in_specs = (
        P("seq", "wa"), P(), P(), P(), P(None, "wa"), P(None, "wa"), P(None, "wa"),
        P(None, "wa"), P("wa"), P("wa", None), P(), P(None, "wa"), P(None, "wa"), P("wa", None),
    )
    out_specs = (P("seq", "wa"), P("seq", "wa", None, None))
    return jax.shard_map(local, mesh=mesh, in_specs=in_specs, out_specs=out_specs, check_vma=False)
```

```python
import jax
import jax.numpy as jnp
from jax import lax
from jax.experimental import pallas as pl
from jax.experimental.pallas import tpu as pltpu
from jax.sharding import PartitionSpec as P

HEAD = 128
GROUP = 64
REQS = 4
CHUNKS = 4
EPS = 1e-06
HIGH = lax.Precision.HIGHEST
MESH = pl.DeviceIdType.MESH
BF = jnp.bfloat16
F32 = jnp.float32
VMEM_BYTES = 58 * 1024 * 1024


def dot(a, b, contract=(1, 0), precision=None):
    return lax.dot_general(
        a, b, (((contract[0],), (contract[1],)), ((), ())), precision=precision,
        preferred_element_type=F32,
    )


def inside(index, count):
    return (index >= 0) & (index < count)


def greet_wa(me, count, barrier):
    for sgn in (1, -1):
        @pl.when(inside(me + sgn, count))
        def _():
            pl.semaphore_signal(barrier, inc=1, device_id={"wa": me + sgn}, device_id_type=MESH)


class Gather:
    def __init__(self, buf, send_sem, recv_sem, me, count, rows):
        self.buf, self.send_sem, self.recv_sem = buf, send_sem, recv_sem
        self.me, self.count, self.rows = me, count, rows

    def copy(self, src, c, sgn, target):
        ref = self.buf.at[src, pl.ds(c * self.rows, self.rows)]
        return pltpu.make_async_remote_copy(
            src_ref=ref, dst_ref=ref,
            send_sem=self.send_sem.at[(sgn + 1) // 2, src, c],
            recv_sem=self.recv_sem.at[src, c],
            device_id={"wa": target}, device_id_type=MESH,
        )

    def own(self, c):
        for sgn in (1, -1):
            @pl.when(inside(self.me + sgn, self.count))
            def _():
                self.copy(self.me, c, sgn, self.me + sgn).start()

    def arrive(self, c):
        for k in range(1, self.count):
            for sgn in (1, -1):
                src = self.me - sgn * k

                @pl.when(inside(src, self.count))
                def _():
                    self.copy(src, c, sgn, self.me - sgn).wait_recv()

                    @pl.when(inside(self.me + sgn, self.count))
                    def _():
                        self.copy(src, c, sgn, self.me + sgn).start()

    def drain(self):
        for c in range(CHUNKS):
            for k in range(self.count):
                for sgn in (1, -1):
                    src = self.me - sgn * k

                    @pl.when(inside(src, self.count) & inside(self.me + sgn, self.count))
                    def _():
                        self.copy(src, c, sgn, self.me + sgn).wait_send()


class Scatter:
    def __init__(self, part, out, came, send_sem, recv_sem, me, count, rows):
        self.part, self.out, self.came = part, out, came
        self.send_sem, self.recv_sem = send_sem, recv_sem
        self.me, self.count, self.rows = me, count, rows
        first = jnp.where(2 * me < count, 1, -1)
        self.ways = (first, -first)

    def copy(self, w, c, sgn, target):
        span = pl.ds(c * self.rows, self.rows)
        way = (sgn + 1) // 2
        return pltpu.make_async_remote_copy(
            src_ref=self.out.at[w, span], dst_ref=self.came.at[way, w, span],
            send_sem=self.send_sem.at[w, c], recv_sem=self.recv_sem.at[way, w, c],
            device_id={"wa": target}, device_id_type=MESH,
        )

    def hop(self, c, relay):
        span = pl.ds(c * self.rows, self.rows)
        me, count = self.me, self.count
        for sgn in self.ways:
            way = (sgn + 1) // 2
            fed = inside(me - sgn, count)
            turn = fed if relay else jnp.logical_not(fed)
            for k in range(count - 1, 0, -1):
                w = me + sgn * k

                @pl.when(inside(w, count) & turn)
                def _():
                    if relay:
                        self.copy(w, c, sgn, me - sgn).wait_recv()
                        self.out[w, span] = (
                            self.part[w, span] + self.came[way, w, span].astype(F32)
                        ).astype(BF)
                    else:
                        self.out[w, span] = self.part[w, span].astype(BF)
                    self.copy(w, c, sgn, me + sgn).start()

    def total(self, c):
        span = pl.ds(c * self.rows, self.rows)
        me, count = self.me, self.count
        for sgn in self.ways:
            way = (sgn + 1) // 2

            @pl.when(inside(me - sgn, count))
            def _():
                self.copy(me, c, sgn, me - sgn).wait_recv()
                self.part[me, span] = self.part[me, span] + self.came[way, me, span].astype(F32)
        return self.part[me, span]

    def drain(self):
        for c in range(CHUNKS):
            for sgn in (1, -1):
                for k in range(1, self.count):
                    w = self.me + sgn * k

                    @pl.when(inside(w, self.count))
                    def _():
                        self.copy(w, c, sgn, self.me + sgn).wait_send()


def rms_chunk(buf, count, c, rows, gain):
    span = pl.ds(c * rows, rows)
    pieces = [buf[s, span].astype(F32) for s in range(count)]
    width = pieces[0].shape[1]
    square = sum(jnp.sum(piece * piece, axis=1, keepdims=True) for piece in pieces)
    rescale = lax.rsqrt(square / (width * count) + EPS)
    return jnp.concatenate(
        [
            (piece * rescale * gain[:, s * width:(s + 1) * width]).astype(BF)
            for s, piece in enumerate(pieces)
        ],
        axis=1,
    )


def silu(v):
    return v / (1.0 + jnp.exp(-v))


def enter_kernel(
    hidden, gain, bias, wq, wf, wi, wg,
    q_out, ld_out, k_out, v_out, g_out,
    buf, vq, vf, vi, vg, w_sem, own_sem, send_sem, recv_sem,
):
    me, count = lax.axis_index("wa"), lax.axis_size("wa")
    rows = hidden.shape[0] // CHUNKS
    loads = [
        pltpu.make_async_copy(src, dst, w_sem.at[i])
        for i, (src, dst) in enumerate(((wq, vq), (wf, vf), (wi, vi), (wg, vg)))
    ]
    mine = pltpu.make_async_copy(hidden, buf.at[me], own_sem)
    mine.start()
    barrier = pltpu.get_barrier_semaphore()
    greet_wa(me, count, barrier)
    mine.wait()
    near = inside(me - 1, count).astype(jnp.int32) + inside(me + 1, count).astype(jnp.int32)
    pl.semaphore_wait(barrier, near)
    ag = Gather(buf, send_sem, recv_sem, me, count, rows)
    ag.own(0)
    ag.own(1)
    for load in loads:
        load.start()
    for c in range(CHUNKS):
        ag.arrive(c)
        if c + 2 < CHUNKS:
            ag.own(c + 2)
        if c == 0:
            for load in loads:
                load.wait()
        span = pl.ds(c * rows, rows)
        normed = rms_chunk(buf, count, c, rows, gain[...])
        q_out[span] = silu(dot(normed, vq[...]))
        logit = dot(normed, vf[...]) + bias[...]
        ld_out[span] = jnp.minimum(logit, 0.0) - jnp.log1p(jnp.exp(-jnp.abs(logit)))
        k_out[span] = 1.0 / (1.0 + jnp.exp(logit))
        v_out[span] = dot(normed, vi[...]).astype(BF)
        g_out[span] = silu(dot(normed, vg[...]))
    ag.drain()


def block_kernel(
    spans, first_ref, q, ld, k, v,
    out, qp, state_out, decay_out, ends, end_decay,
    state, decay,
):
    heads = q.shape[1] // HEAD
    blocks = q.shape[0] // GROUP
    state[...] = jnp.zeros_like(state)
    decay[...] = jnp.ones_like(decay)
    ends[...] = jnp.zeros_like(ends)
    end_decay[...] = jnp.zeros_like(end_decay)
    below = lax.broadcasted_iota(jnp.int32, (GROUP, GROUP), 0)
    across = lax.broadcasted_iota(jnp.int32, (GROUP, GROUP), 1)
    causal = below >= across
    lower = causal.astype(F32)
    column = lax.broadcasted_iota(jnp.int32, (GROUP, 1), 0)
    line = lax.broadcasted_iota(jnp.int32, (1, GROUP), 1)

    def began(position):
        return sum((spans[r, 0] <= position).astype(jnp.int32) for r in range(REQS))

    def body(n, carry):
        rows = pl.ds(pl.multiple_of(n * GROUP, GROUP), GROUP)
        base = first_ref[0] + n * GROUP
        cum = dot(lower, ld[rows], precision=HIGH)
        qt = q[rows] * jnp.exp(cum)
        kt = k[rows] * jnp.exp(-cum)
        vb = v[rows]
        seg = began(base + column)
        mask = causal & (seg == began(base + line))
        prev, last = began(base - 1), began(base + GROUP - 1)
        surviving = (seg == prev).astype(F32)
        tail = (seg == last).astype(F32)
        alive = (last == prev).astype(F32)
        for r in range(REQS):
            within = spans[r, 1] - 1 - base

            @pl.when((within >= 0) & (within < GROUP))
            def _():
                upto = ((column <= within) & (seg == r + 1)).astype(F32)
                alive_end = (prev == r + 1).astype(F32)
                at_end = jnp.exp(
                    jnp.sum(jnp.where(column == within, cum, 0.0), axis=0, keepdims=True)
                )
                for h in range(heads):
                    hs = slice(h * HEAD, (h + 1) * HEAD)
                    partial = dot(vb[:, hs], (kt[:, hs] * upto).astype(BF), (0, 0))
                    ends[r, h] = at_end[:, hs] * (alive_end * state[h] + partial)
                    end_decay[r, h:h + 1] = at_end[:, hs] * alive_end * decay[h:h + 1]

        for h in range(heads):
            hs = slice(h * HEAD, (h + 1) * HEAD)
            qh, vh = qt[:, hs].astype(BF), vb[:, hs]
            scores = dot(qh, kt[:, hs].astype(BF), (1, 1))
            scores = jnp.where(mask, scores, 0.0).astype(BF)
            held, shrunk = state[h], decay[h:h + 1]
            out[rows, hs] = dot(scores, vh) + surviving * dot(qh, held.astype(BF), (1, 1))
            qp[rows, hs] = (qt[:, hs] * surviving * shrunk).astype(BF)
            fresh = dot(vh, (kt[:, hs] * tail).astype(BF), (0, 0))
            full = jnp.exp(cum[GROUP - 1:GROUP, hs])
            state[h] = full * (alive * held + fresh)
            decay[h:h + 1] = shrunk * (full * alive)
        return carry

    lax.fori_loop(0, blocks, body, 0)
    state_out[...] = state[...].astype(BF)
    decay_out[...] = decay[...]


def leave_kernel(
    owners, hidden, out_local, qp, g, state, decay, ends, end_decay, gain, wo, wgate, wup, wdown,
    y_out, handed_out,
    vo, vgate, vup, vdown, part1, part2, out1, out2, came1, came2, buf,
    states, decays, incoming, end_mine, end_out, end_came,
    w_sem, rs1_send, rs1_recv, rs2_send, rs2_recv, ag_send, ag_recv,
    st_send, st_recv, de_send, de_recv, en_send, en_recv,
):
    me, count = lax.axis_index("wa"), lax.axis_size("wa")
    place, places = lax.axis_index("seq"), lax.axis_size("seq")
    rows = hidden.shape[0] // CHUNKS
    width = hidden.shape[1]
    heads = width // HEAD
    loads = [
        pltpu.make_async_copy(src, dst, w_sem.at[i])
        for i, (src, dst) in enumerate(((wo, vo), (wgate, vgate), (wup, vup), (wdown, vdown)))
    ]
    barrier = pltpu.get_barrier_semaphore()
    greet_wa(me, count, barrier)

    def others(act):
        def step(j, carry):
            act(lax.rem(place + j, places))
            return carry
        lax.fori_loop(1, places, step, 0)

    others(lambda peer: pl.semaphore_signal(
        barrier, inc=1, device_id={"seq": peer}, device_id_type=MESH))
    near = inside(me - 1, count).astype(jnp.int32) + inside(me + 1, count).astype(jnp.int32)
    pl.semaphore_wait(barrier, near + (places - 1))

    def state_copy(source, peer, send):
        return pltpu.make_async_remote_copy(
            src_ref=state, dst_ref=states.at[source], send_sem=st_send.at[send],
            recv_sem=st_recv.at[source], device_id={"seq": peer}, device_id_type=MESH)

    def decay_copy(source, peer, send):
        return pltpu.make_async_remote_copy(
            src_ref=decay, dst_ref=decays.at[source], send_sem=de_send.at[send],
            recv_sem=de_recv.at[source], device_id={"seq": peer}, device_id_type=MESH)

    def end_copy(source, peer, send):
        return pltpu.make_async_remote_copy(
            src_ref=end_out.at[send], dst_ref=end_came.at[source], send_sem=en_send.at[send],
            recv_sem=en_recv.at[source], device_id={"seq": peer}, device_id_type=MESH)

    def later(act):
        def step(peer, carry):
            act(peer)
            return carry
        lax.fori_loop(place + 1, places, step, 0)

    def push(peer):
        state_copy(place, peer, peer).start()
        decay_copy(place, peer, peer).start()

    later(push)
    for load in loads:
        load.start()
    incoming[...] = jnp.zeros_like(incoming)

    def join(p, carry):
        state_copy(p, p, p).wait_recv()
        decay_copy(p, p, p).wait_recv()
        for h in range(heads):
            incoming[h] = incoming[h] * decays[p, h:h + 1] + states[p, h].astype(F32)
        return carry

    lax.fori_loop(0, place, join, 0)
    loads[0].wait()

    rs1 = Scatter(part1, out1, came1, rs1_send, rs1_recv, me, count, rows)
    rs2 = Scatter(part2, out2, came2, rs2_send, rs2_recv, me, count, rows)
    ag = Gather(buf, ag_send, ag_recv, me, count, rows)

    def mix(c):
        span = pl.ds(c * rows, rows)
        mixed = []
        for h in range(heads):
            hs = slice(h * HEAD, (h + 1) * HEAD)
            o = out_local[span, hs] + dot(qp[span, hs], incoming[h].astype(BF), (1, 1))
            rescale = lax.rsqrt(jnp.mean(o * o, axis=1, keepdims=True) + EPS)
            mixed.append((o * rescale * g[span, hs]).astype(BF))
        mixed = jnp.concatenate(mixed, axis=1)
        for w in range(count):
            part1[w, span] = dot(mixed, vo[:, w * width:(w + 1) * width])

    def settle(c):
        span = pl.ds(c * rows, rows)
        buf[me, span] = (hidden[span].astype(F32) + rs1.total(c)).astype(BF)
        ag.own(c)

    def feed(c):
        span = pl.ds(c * rows, rows)
        ag.arrive(c)
        normed = rms_chunk(buf, count, c, rows, gain[...])
        units = (silu(dot(normed, vgate[...])) * dot(normed, vup[...])).astype(BF)
        for w in range(count):
            part2[w, span] = dot(units, vdown[:, w * width:(w + 1) * width])

    def finish(c):
        span = pl.ds(c * rows, rows)
        y_out[span] = (buf[me, span].astype(F32) + rs2.total(c)).astype(BF)

    def hand_over():
        for r in range(REQS):
            for h in range(heads):
                end_mine[r, h] = ends[r, h] + end_decay[r, h:h + 1] * incoming[h]

        def fill(peer, carry):
            picks = [(owners[r] == peer).astype(F32) for r in range(REQS)]
            for h in range(heads):
                end_out[peer, h] = sum(picks[r] * end_mine[r, h] for r in range(REQS)).astype(BF)
            return carry

        lax.fori_loop(0, places, fill, 0)
        others(lambda peer: end_copy(place, peer, peer).start())

    mix(0)
    rs1.hop(0, False)
    mix(1)
    rs1.hop(1, False)
    rs1.hop(0, True)
    mix(2)
    rs1.hop(2, False)
    settle(0)
    rs1.hop(1, True)
    mix(3)
    rs1.hop(3, False)
    settle(1)
    rs1.hop(2, True)
    hand_over()
    for load in loads[1:]:
        load.wait()
    feed(0)
    rs2.hop(0, False)
    settle(2)
    rs1.hop(3, True)
    feed(1)
    rs2.hop(1, False)
    settle(3)
    rs2.hop(0, True)
    feed(2)
    rs2.hop(2, False)
    finish(0)
    rs2.hop(1, True)
    feed(3)
    rs2.hop(3, False)
    finish(1)
    rs2.hop(2, True)
    finish(2)
    rs2.hop(3, True)
    finish(3)

    others(lambda peer: end_copy(peer, peer, peer).wait_recv())
    end_came[place] = end_out[place]
    for h in range(heads):
        def gather_end(p, total):
            return total + end_came[p, h].astype(F32)
        handed_out[0, h] = lax.fori_loop(
            0, places, gather_end, jnp.zeros((HEAD, HEAD), F32)).T
    others(lambda peer: end_copy(place, peer, peer).wait_send())

    def sent(peer):
        state_copy(place, peer, peer).wait_send()
        decay_copy(place, peer, peer).wait_send()

    later(sent)
    rs1.drain()
    rs2.drain()
    ag.drain()


def local(
    hidden_in, request_spans, owners, mixer_gain, query_weight, forget_weight, input_weight,
    gate_weight, forget_bias, output_weight, swiglu_gain, swiglu_gate, swiglu_up, swiglu_down,
):
    count, places = lax.axis_size("wa"), lax.axis_size("seq")
    tok, width = hidden_in.shape
    heads = width // HEAD
    depth = query_weight.shape[0]
    ff = swiglu_gate.shape[1]
    vmem = pl.BlockSpec(memory_space=pltpu.VMEM)
    smem = pl.BlockSpec(memory_space=pltpu.SMEM)
    hbm = pl.BlockSpec(memory_space=pl.ANY)
    DMA = pltpu.SemaphoreType.DMA

    q, ld, k, v, g = pl.pallas_call(
        enter_kernel,
        out_shape=[jax.ShapeDtypeStruct((tok, width), t) for t in (F32, F32, F32, BF, F32)],
        in_specs=[vmem] * 3 + [hbm] * 4,
        out_specs=[vmem] * 5,
        scratch_shapes=[pltpu.VMEM((count, tok, width), BF)]
        + [pltpu.VMEM((depth, width), BF)] * 4
        + [DMA((4,)), DMA, DMA((2, count, CHUNKS)), DMA((count, CHUNKS))],
        compiler_params=pltpu.CompilerParams(
            collective_id=0, has_side_effects=True, vmem_limit_bytes=VMEM_BYTES),
        name="enter",
    )(
        hidden_in, mixer_gain[None], forget_bias[None],
        query_weight, forget_weight, input_weight, gate_weight,
    )

    first = (lax.axis_index("seq") * tok).astype(jnp.int32)[None]
    out_local, qp, state, decay, ends, end_decay = pl.pallas_call(
        block_kernel,
        out_shape=[
            jax.ShapeDtypeStruct((tok, width), F32),
            jax.ShapeDtypeStruct((tok, width), BF),
            jax.ShapeDtypeStruct((heads, HEAD, HEAD), BF),
            jax.ShapeDtypeStruct((heads, HEAD), F32),
            jax.ShapeDtypeStruct((REQS, heads, HEAD, HEAD), F32),
            jax.ShapeDtypeStruct((REQS, heads, HEAD), F32),
        ],
        in_specs=[smem, smem] + [vmem] * 4,
        out_specs=[vmem] * 6,
        scratch_shapes=[pltpu.VMEM((heads, HEAD, HEAD), F32), pltpu.VMEM((heads, HEAD), F32)],
        compiler_params=pltpu.CompilerParams(vmem_limit_bytes=VMEM_BYTES),
        name="blocks",
    )(request_spans, first, q, ld, k, v)

    y, handed = pl.pallas_call(
        leave_kernel,
        out_shape=[
            jax.ShapeDtypeStruct((tok, width), BF),
            jax.ShapeDtypeStruct((1, heads, HEAD, HEAD), F32),
        ],
        in_specs=[smem] + [vmem] * 9 + [hbm] * 4,
        out_specs=[vmem] * 2,
        scratch_shapes=[
            pltpu.VMEM((width, depth), BF),
            pltpu.VMEM((depth, ff), BF),
            pltpu.VMEM((depth, ff), BF),
            pltpu.VMEM((ff, depth), BF),
            pltpu.VMEM((count, tok, width), F32),
            pltpu.VMEM((count, tok, width), F32),
            pltpu.VMEM((count, tok, width), BF),
            pltpu.VMEM((count, tok, width), BF),
            pltpu.VMEM((2, count, tok, width), BF),
            pltpu.VMEM((2, count, tok, width), BF),
            pltpu.VMEM((count, tok, width), BF),
            pltpu.VMEM((places, heads, HEAD, HEAD), BF),
            pltpu.VMEM((places, heads, HEAD), F32),
            pltpu.VMEM((heads, HEAD, HEAD), F32),
            pltpu.VMEM((REQS, heads, HEAD, HEAD), F32),
            pltpu.VMEM((places, heads, HEAD, HEAD), BF),
            pltpu.VMEM((places, heads, HEAD, HEAD), BF),
            DMA((4,)),
            DMA((count, CHUNKS)), DMA((2, count, CHUNKS)),
            DMA((count, CHUNKS)), DMA((2, count, CHUNKS)),
            DMA((2, count, CHUNKS)), DMA((count, CHUNKS)),
            DMA((places,)), DMA((places,)), DMA((places,)), DMA((places,)),
            DMA((places,)), DMA((places,)),
        ],
        compiler_params=pltpu.CompilerParams(
            collective_id=1, has_side_effects=True, vmem_limit_bytes=VMEM_BYTES),
        name="leave",
    )(
        owners, hidden_in, out_local, qp, g, state, decay, ends, end_decay,
        swiglu_gain[None], output_weight, swiglu_gate, swiglu_up, swiglu_down,
    )
    return y, handed


def solution(mesh):
    in_specs = (
        P("seq", "wa"), P(), P(), P(), P(None, "wa"), P(None, "wa"), P(None, "wa"),
        P(None, "wa"), P("wa"), P("wa", None), P(), P(None, "wa"), P(None, "wa"), P("wa", None),
    )
    out_specs = (P("seq", "wa"), P("seq", "wa", None, None))
    return jax.shard_map(local, mesh=mesh, in_specs=in_specs, out_specs=out_specs, check_vma=False)
```

```python
import jax
import jax.numpy as jnp
from jax import lax
from jax.experimental import pallas as pl
from jax.experimental.pallas import tpu as pltpu
from jax.sharding import PartitionSpec as P

HEAD = 128
GROUP = 64
REQS = 4
CHUNKS = 4
EPS = 1e-06
HIGH = lax.Precision.HIGHEST
MESH = pl.DeviceIdType.MESH
BF = jnp.bfloat16
F32 = jnp.float32
VMEM_BYTES = 58 * 1024 * 1024


def dot(a, b, contract=(1, 0), precision=None):
    return lax.dot_general(
        a, b, (((contract[0],), (contract[1],)), ((), ())), precision=precision,
        preferred_element_type=F32,
    )


def inside(index, count):
    return (index >= 0) & (index < count)


def greet_wa(me, count, barrier):
    for sgn in (1, -1):
        @pl.when(inside(me + sgn, count))
        def _():
            pl.semaphore_signal(barrier, inc=1, device_id={"wa": me + sgn}, device_id_type=MESH)


class Gather:
    def __init__(self, buf, send_sem, recv_sem, me, count, rows):
        self.buf, self.send_sem, self.recv_sem = buf, send_sem, recv_sem
        self.me, self.count, self.rows = me, count, rows

    def copy(self, src, c, sgn, target):
        ref = self.buf.at[src, pl.ds(c * self.rows, self.rows)]
        return pltpu.make_async_remote_copy(
            src_ref=ref, dst_ref=ref,
            send_sem=self.send_sem.at[(sgn + 1) // 2, src, c],
            recv_sem=self.recv_sem.at[src, c],
            device_id={"wa": target}, device_id_type=MESH,
        )

    def own(self, c):
        for sgn in (1, -1):
            @pl.when(inside(self.me + sgn, self.count))
            def _():
                self.copy(self.me, c, sgn, self.me + sgn).start()

    def arrive(self, c):
        for k in range(1, self.count):
            for sgn in (1, -1):
                src = self.me - sgn * k

                @pl.when(inside(src, self.count))
                def _():
                    self.copy(src, c, sgn, self.me - sgn).wait_recv()

                    @pl.when(inside(self.me + sgn, self.count))
                    def _():
                        self.copy(src, c, sgn, self.me + sgn).start()

    def drain(self):
        for c in range(CHUNKS):
            for k in range(self.count):
                for sgn in (1, -1):
                    src = self.me - sgn * k

                    @pl.when(inside(src, self.count) & inside(self.me + sgn, self.count))
                    def _():
                        self.copy(src, c, sgn, self.me + sgn).wait_send()


class Scatter:
    def __init__(self, part, out, came, send_sem, recv_sem, me, count, rows):
        self.part, self.out, self.came = part, out, came
        self.send_sem, self.recv_sem = send_sem, recv_sem
        self.me, self.count, self.rows = me, count, rows
        first = jnp.where(2 * me < count, 1, -1)
        self.ways = (first, -first)

    def copy(self, w, c, sgn, target):
        span = pl.ds(c * self.rows, self.rows)
        way = (sgn + 1) // 2
        return pltpu.make_async_remote_copy(
            src_ref=self.out.at[w, span], dst_ref=self.came.at[way, w, span],
            send_sem=self.send_sem.at[w, c], recv_sem=self.recv_sem.at[way, w, c],
            device_id={"wa": target}, device_id_type=MESH,
        )

    def hop(self, c, relay):
        span = pl.ds(c * self.rows, self.rows)
        me, count = self.me, self.count
        for sgn in self.ways:
            way = (sgn + 1) // 2
            fed = inside(me - sgn, count)
            turn = fed if relay else jnp.logical_not(fed)
            if c > 0 and not relay:
                self.sent(c - 1, sgn, turn)
            for k in range(count - 1, 0, -1):
                w = me + sgn * k

                @pl.when(inside(w, count) & turn)
                def _():
                    if relay:
                        self.copy(w, c, sgn, me - sgn).wait_recv()
                        self.out[w, span] = (
                            self.part[w, span] + self.came[way, w, span].astype(F32)
                        ).astype(BF)
                    else:
                        self.out[w, span] = self.part[w, span].astype(BF)
                    self.copy(w, c, sgn, me + sgn).start()

    def total(self, c):
        span = pl.ds(c * self.rows, self.rows)
        me, count = self.me, self.count
        for sgn in self.ways:
            way = (sgn + 1) // 2

            @pl.when(inside(me - sgn, count))
            def _():
                self.copy(me, c, sgn, me - sgn).wait_recv()
                self.part[me, span] = self.part[me, span] + self.came[way, me, span].astype(F32)
        return self.part[me, span]

    def sent(self, c, sgn, turn):
        for k in range(1, self.count):
            w = self.me + sgn * k

            @pl.when(inside(w, self.count) & turn)
            def _():
                self.copy(w, c, sgn, self.me + sgn).wait_send()

    def drain(self):
        for sgn in (1, -1):
            fed = inside(self.me - sgn, self.count)
            for c in range(CHUNKS):
                self.sent(c, sgn, fed)
            self.sent(CHUNKS - 1, sgn, jnp.logical_not(fed))


def rms_chunk(buf, count, c, rows, gain):
    span = pl.ds(c * rows, rows)
    pieces = [buf[s, span].astype(F32) for s in range(count)]
    width = pieces[0].shape[1]
    square = sum(jnp.sum(piece * piece, axis=1, keepdims=True) for piece in pieces)
    rescale = lax.rsqrt(square / (width * count) + EPS)
    return jnp.concatenate(
        [
            (piece * rescale * gain[:, s * width:(s + 1) * width]).astype(BF)
            for s, piece in enumerate(pieces)
        ],
        axis=1,
    )


def silu(v):
    return v / (1.0 + jnp.exp(-v))


def enter_kernel(
    hidden, gain, bias, wq, wf, wi, wg,
    q_out, ld_out, k_out, v_out, g_out,
    buf, vq, vf, vi, vg, w_sem, own_sem, send_sem, recv_sem,
):
    me, count = lax.axis_index("wa"), lax.axis_size("wa")
    rows = hidden.shape[0] // CHUNKS
    loads = [
        pltpu.make_async_copy(src, dst, w_sem.at[i])
        for i, (src, dst) in enumerate(((wq, vq), (wf, vf), (wi, vi), (wg, vg)))
    ]
    mine = pltpu.make_async_copy(hidden, buf.at[me], own_sem)
    mine.start()
    barrier = pltpu.get_barrier_semaphore()
    greet_wa(me, count, barrier)
    mine.wait()
    near = inside(me - 1, count).astype(jnp.int32) + inside(me + 1, count).astype(jnp.int32)
    pl.semaphore_wait(barrier, near)
    ag = Gather(buf, send_sem, recv_sem, me, count, rows)
    ag.own(0)
    ag.own(1)
    for load in loads:
        load.start()
    for c in range(CHUNKS):
        ag.arrive(c)
        if c + 2 < CHUNKS:
            ag.own(c + 2)
        if c == 0:
            for load in loads:
                load.wait()
        span = pl.ds(c * rows, rows)
        normed = rms_chunk(buf, count, c, rows, gain[...])
        q_out[span] = silu(dot(normed, vq[...]))
        logit = dot(normed, vf[...]) + bias[...]
        ld_out[span] = jnp.minimum(logit, 0.0) - jnp.log1p(jnp.exp(-jnp.abs(logit)))
        k_out[span] = 1.0 / (1.0 + jnp.exp(logit))
        v_out[span] = dot(normed, vi[...]).astype(BF)
        g_out[span] = silu(dot(normed, vg[...]))
    ag.drain()


def block_kernel(
    spans, first_ref, q, ld, k, v,
    out, qp, state_out, decay_out, ends, end_decay,
    state, decay,
):
    heads = q.shape[1] // HEAD
    blocks = q.shape[0] // GROUP
    state[...] = jnp.zeros_like(state)
    decay[...] = jnp.ones_like(decay)
    ends[...] = jnp.zeros_like(ends)
    end_decay[...] = jnp.zeros_like(end_decay)
    below = lax.broadcasted_iota(jnp.int32, (GROUP, GROUP), 0)
    across = lax.broadcasted_iota(jnp.int32, (GROUP, GROUP), 1)
    causal = below >= across
    lower = causal.astype(F32)
    column = lax.broadcasted_iota(jnp.int32, (GROUP, 1), 0)
    line = lax.broadcasted_iota(jnp.int32, (1, GROUP), 1)

    def began(position):
        return sum((spans[r, 0] <= position).astype(jnp.int32) for r in range(REQS))

    def body(n, carry):
        rows = pl.ds(pl.multiple_of(n * GROUP, GROUP), GROUP)
        base = first_ref[0] + n * GROUP
        cum = dot(lower, ld[rows], precision=HIGH)
        qt = q[rows] * jnp.exp(cum)
        kt = k[rows] * jnp.exp(-cum)
        vb = v[rows]
        seg = began(base + column)
        mask = causal & (seg == began(base + line))
        prev, last = began(base - 1), began(base + GROUP - 1)
        surviving = (seg == prev).astype(F32)
        tail = (seg == last).astype(F32)
        alive = (last == prev).astype(F32)
        for r in range(REQS):
            within = spans[r, 1] - 1 - base

            @pl.when((within >= 0) & (within < GROUP))
            def _():
                upto = ((column <= within) & (seg == r + 1)).astype(F32)
                alive_end = (prev == r + 1).astype(F32)
                at_end = jnp.exp(
                    jnp.sum(jnp.where(column == within, cum, 0.0), axis=0, keepdims=True)
                )
                for h in range(heads):
                    hs = slice(h * HEAD, (h + 1) * HEAD)
                    partial = dot(vb[:, hs], (kt[:, hs] * upto).astype(BF), (0, 0))
                    ends[r, h] = at_end[:, hs] * (alive_end * state[h] + partial)
                    end_decay[r, h:h + 1] = at_end[:, hs] * alive_end * decay[h:h + 1]

        for h in range(heads):
            hs = slice(h * HEAD, (h + 1) * HEAD)
            qh, vh = qt[:, hs].astype(BF), vb[:, hs]
            scores = dot(qh, kt[:, hs].astype(BF), (1, 1))
            scores = jnp.where(mask, scores, 0.0).astype(BF)
            held, shrunk = state[h], decay[h:h + 1]
            out[rows, hs] = dot(scores, vh) + surviving * dot(qh, held.astype(BF), (1, 1))
            qp[rows, hs] = (qt[:, hs] * surviving * shrunk).astype(BF)
            fresh = dot(vh, (kt[:, hs] * tail).astype(BF), (0, 0))
            full = jnp.exp(cum[GROUP - 1:GROUP, hs])
            state[h] = full * (alive * held + fresh)
            decay[h:h + 1] = shrunk * (full * alive)
        return carry

    lax.fori_loop(0, blocks, body, 0)
    state_out[...] = state[...].astype(BF)
    decay_out[...] = decay[...]


def leave_kernel(
    owners, hidden, out_local, qp, g, state, decay, ends, end_decay, gain, wo, wgate, wup, wdown,
    y_out, handed_out,
    vo, vgate, vup, vdown, part1, part2, out1, out2, came1, came2, buf,
    states, decays, incoming, end_mine, end_out, end_came,
    w_sem, rs1_send, rs1_recv, rs2_send, rs2_recv, ag_send, ag_recv,
    st_send, st_recv, de_send, de_recv, en_send, en_recv,
):
    me, count = lax.axis_index("wa"), lax.axis_size("wa")
    place, places = lax.axis_index("seq"), lax.axis_size("seq")
    rows = hidden.shape[0] // CHUNKS
    width = hidden.shape[1]
    heads = width // HEAD
    loads = [
        pltpu.make_async_copy(src, dst, w_sem.at[i])
        for i, (src, dst) in enumerate(((wo, vo), (wgate, vgate), (wup, vup), (wdown, vdown)))
    ]
    barrier = pltpu.get_barrier_semaphore()
    greet_wa(me, count, barrier)

    def others(act):
        def step(j, carry):
            act(lax.rem(place + j, places))
            return carry
        lax.fori_loop(1, places, step, 0)

    others(lambda peer: pl.semaphore_signal(
        barrier, inc=1, device_id={"seq": peer}, device_id_type=MESH))
    near = inside(me - 1, count).astype(jnp.int32) + inside(me + 1, count).astype(jnp.int32)
    pl.semaphore_wait(barrier, near + (places - 1))

    def state_copy(source, peer, send):
        return pltpu.make_async_remote_copy(
            src_ref=state, dst_ref=states.at[source], send_sem=st_send.at[send],
            recv_sem=st_recv.at[source], device_id={"seq": peer}, device_id_type=MESH)

    def decay_copy(source, peer, send):
        return pltpu.make_async_remote_copy(
            src_ref=decay, dst_ref=decays.at[source], send_sem=de_send.at[send],
            recv_sem=de_recv.at[source], device_id={"seq": peer}, device_id_type=MESH)

    def end_copy(source, peer, send):
        return pltpu.make_async_remote_copy(
            src_ref=end_out.at[send], dst_ref=end_came.at[source], send_sem=en_send.at[send],
            recv_sem=en_recv.at[source], device_id={"seq": peer}, device_id_type=MESH)

    def later(act):
        def step(peer, carry):
            act(peer)
            return carry
        lax.fori_loop(place + 1, places, step, 0)

    def push(peer):
        state_copy(place, peer, peer).start()
        decay_copy(place, peer, peer).start()

    later(push)
    for load in loads:
        load.start()
    incoming[...] = jnp.zeros_like(incoming)

    def join(p, carry):
        state_copy(p, p, p).wait_recv()
        decay_copy(p, p, p).wait_recv()
        for h in range(heads):
            incoming[h] = incoming[h] * decays[p, h:h + 1] + states[p, h].astype(F32)
        return carry

    lax.fori_loop(0, place, join, 0)
    loads[0].wait()

    rs1 = Scatter(part1, out1, came1, rs1_send, rs1_recv, me, count, rows)
    rs2 = Scatter(part2, out2, came2, rs2_send, rs2_recv, me, count, rows)
    ag = Gather(buf, ag_send, ag_recv, me, count, rows)

    def mix(c):
        span = pl.ds(c * rows, rows)
        mixed = []
        for h in range(heads):
            hs = slice(h * HEAD, (h + 1) * HEAD)
            o = out_local[span, hs] + dot(qp[span, hs], incoming[h].astype(BF), (1, 1))
            rescale = lax.rsqrt(jnp.mean(o * o, axis=1, keepdims=True) + EPS)
            mixed.append((o * rescale * g[span, hs]).astype(BF))
        mixed = jnp.concatenate(mixed, axis=1)
        for w in range(count):
            part1[w, span] = dot(mixed, vo[:, w * width:(w + 1) * width])

    def settle(c):
        span = pl.ds(c * rows, rows)
        buf[me, span] = (hidden[span].astype(F32) + rs1.total(c)).astype(BF)
        ag.own(c)

    def feed(c):
        span = pl.ds(c * rows, rows)
        ag.arrive(c)
        normed = rms_chunk(buf, count, c, rows, gain[...])
        units = (silu(dot(normed, vgate[...])) * dot(normed, vup[...])).astype(BF)
        for w in range(count):
            part2[w, span] = dot(units, vdown[:, w * width:(w + 1) * width])

    def finish(c):
        span = pl.ds(c * rows, rows)
        y_out[span] = (buf[me, span].astype(F32) + rs2.total(c)).astype(BF)

    def hand_over():
        for r in range(REQS):
            for h in range(heads):
                end_mine[r, h] = ends[r, h] + end_decay[r, h:h + 1] * incoming[h]

        def fill(peer, carry):
            picks = [(owners[r] == peer).astype(F32) for r in range(REQS)]
            for h in range(heads):
                end_out[peer, h] = sum(picks[r] * end_mine[r, h] for r in range(REQS)).astype(BF)
            return carry

        lax.fori_loop(0, places, fill, 0)
        others(lambda peer: end_copy(place, peer, peer).start())

    mix(0)
    rs1.hop(0, False)
    mix(1)
    rs1.hop(1, False)
    rs1.hop(0, True)
    mix(2)
    rs1.hop(2, False)
    settle(0)
    rs1.hop(1, True)
    mix(3)
    rs1.hop(3, False)
    settle(1)
    rs1.hop(2, True)
    hand_over()
    for load in loads[1:]:
        load.wait()
    feed(0)
    rs2.hop(0, False)
    settle(2)
    rs1.hop(3, True)
    feed(1)
    rs2.hop(1, False)
    settle(3)
    rs2.hop(0, True)
    feed(2)
    rs2.hop(2, False)
    finish(0)
    rs2.hop(1, True)
    feed(3)
    rs2.hop(3, False)
    finish(1)
    rs2.hop(2, True)
    finish(2)
    rs2.hop(3, True)
    finish(3)

    others(lambda peer: end_copy(peer, peer, peer).wait_recv())
    end_came[place] = end_out[place]
    for h in range(heads):
        def gather_end(p, total):
            return total + end_came[p, h].astype(F32)
        handed_out[0, h] = lax.fori_loop(
            0, places, gather_end, jnp.zeros((HEAD, HEAD), F32)).T
    others(lambda peer: end_copy(place, peer, peer).wait_send())

    def sent(peer):
        state_copy(place, peer, peer).wait_send()
        decay_copy(place, peer, peer).wait_send()

    later(sent)
    rs1.drain()
    rs2.drain()
    ag.drain()


def local(
    hidden_in, request_spans, owners, mixer_gain, query_weight, forget_weight, input_weight,
    gate_weight, forget_bias, output_weight, swiglu_gain, swiglu_gate, swiglu_up, swiglu_down,
):
    count, places = lax.axis_size("wa"), lax.axis_size("seq")
    tok, width = hidden_in.shape
    heads = width // HEAD
    depth = query_weight.shape[0]
    ff = swiglu_gate.shape[1]
    vmem = pl.BlockSpec(memory_space=pltpu.VMEM)
    smem = pl.BlockSpec(memory_space=pltpu.SMEM)
    hbm = pl.BlockSpec(memory_space=pl.ANY)
    DMA = pltpu.SemaphoreType.DMA

    q, ld, k, v, g = pl.pallas_call(
        enter_kernel,
        out_shape=[jax.ShapeDtypeStruct((tok, width), t) for t in (F32, F32, F32, BF, F32)],
        in_specs=[vmem] * 3 + [hbm] * 4,
        out_specs=[vmem] * 5,
        scratch_shapes=[pltpu.VMEM((count, tok, width), BF)]
        + [pltpu.VMEM((depth, width), BF)] * 4
        + [DMA((4,)), DMA, DMA((2, count, CHUNKS)), DMA((count, CHUNKS))],
        compiler_params=pltpu.CompilerParams(
            collective_id=0, has_side_effects=True, vmem_limit_bytes=VMEM_BYTES),
        name="enter",
    )(
        hidden_in, mixer_gain[None], forget_bias[None],
        query_weight, forget_weight, input_weight, gate_weight,
    )

    first = (lax.axis_index("seq") * tok).astype(jnp.int32)[None]
    out_local, qp, state, decay, ends, end_decay = pl.pallas_call(
        block_kernel,
        out_shape=[
            jax.ShapeDtypeStruct((tok, width), F32),
            jax.ShapeDtypeStruct((tok, width), BF),
            jax.ShapeDtypeStruct((heads, HEAD, HEAD), BF),
            jax.ShapeDtypeStruct((heads, HEAD), F32),
            jax.ShapeDtypeStruct((REQS, heads, HEAD, HEAD), F32),
            jax.ShapeDtypeStruct((REQS, heads, HEAD), F32),
        ],
        in_specs=[smem, smem] + [vmem] * 4,
        out_specs=[vmem] * 6,
        scratch_shapes=[pltpu.VMEM((heads, HEAD, HEAD), F32), pltpu.VMEM((heads, HEAD), F32)],
        compiler_params=pltpu.CompilerParams(vmem_limit_bytes=VMEM_BYTES),
        name="blocks",
    )(request_spans, first, q, ld, k, v)

    y, handed = pl.pallas_call(
        leave_kernel,
        out_shape=[
            jax.ShapeDtypeStruct((tok, width), BF),
            jax.ShapeDtypeStruct((1, heads, HEAD, HEAD), F32),
        ],
        in_specs=[smem] + [vmem] * 9 + [hbm] * 4,
        out_specs=[vmem] * 2,
        scratch_shapes=[
            pltpu.VMEM((width, depth), BF),
            pltpu.VMEM((depth, ff), BF),
            pltpu.VMEM((depth, ff), BF),
            pltpu.VMEM((ff, depth), BF),
            pltpu.VMEM((count, tok, width), F32),
            pltpu.VMEM((count, tok, width), F32),
            pltpu.VMEM((count, tok, width), BF),
            pltpu.VMEM((count, tok, width), BF),
            pltpu.VMEM((2, count, tok, width), BF),
            pltpu.VMEM((2, count, tok, width), BF),
            pltpu.VMEM((count, tok, width), BF),
            pltpu.VMEM((places, heads, HEAD, HEAD), BF),
            pltpu.VMEM((places, heads, HEAD), F32),
            pltpu.VMEM((heads, HEAD, HEAD), F32),
            pltpu.VMEM((REQS, heads, HEAD, HEAD), F32),
            pltpu.VMEM((places, heads, HEAD, HEAD), BF),
            pltpu.VMEM((places, heads, HEAD, HEAD), BF),
            DMA((4,)),
            DMA((count, CHUNKS)), DMA((2, count, CHUNKS)),
            DMA((count, CHUNKS)), DMA((2, count, CHUNKS)),
            DMA((2, count, CHUNKS)), DMA((count, CHUNKS)),
            DMA((places,)), DMA((places,)), DMA((places,)), DMA((places,)),
            DMA((places,)), DMA((places,)),
        ],
        compiler_params=pltpu.CompilerParams(
            collective_id=1, has_side_effects=True, vmem_limit_bytes=VMEM_BYTES),
        name="leave",
    )(
        owners, hidden_in, out_local, qp, g, state, decay, ends, end_decay,
        swiglu_gain[None], output_weight, swiglu_gate, swiglu_up, swiglu_down,
    )
    return y, handed


def solution(mesh):
    in_specs = (
        P("seq", "wa"), P(), P(), P(), P(None, "wa"), P(None, "wa"), P(None, "wa"),
        P(None, "wa"), P("wa"), P("wa", None), P(), P(None, "wa"), P(None, "wa"), P("wa", None),
    )
    out_specs = (P("seq", "wa"), P("seq", "wa", None, None))
    return jax.shard_map(local, mesh=mesh, in_specs=in_specs, out_specs=out_specs, check_vma=False)
```
